32 devices in a mesh: ctx: 2 (over y), head: 4 (over x, core), dp: 4 (over z).
Axes of the slice: x: 2, y: 2, z: 4, core: 2. Of those that a mesh axis runs over, the one named last changes fastest.
Arguments:
- query_states: bfloat16 [4096, 8192], P(('dp', 'ctx'), 'head'), parts along dimension 0, may hold values from -6 to 6
- key_states: bfloat16 [4096, 1024], P(('dp', 'ctx'), 'head'), parts along dimension 0, may hold values from -6 to 6
- value_state_rows: bfloat16 [4096, 1024], P(('dp', 'ctx'), 'head'), parts along dimension 0, may hold values from -6 to 6
- grad_out: bfloat16 [4096, 8192], P(('dp', 'ctx'), 'head'), parts along dimension 0, may hold values from -6 to 6
- vis_blocks: int32 [32, 6], P('dp'), parts along dimension 0, may hold values from 0 to 7, as said below
- vis_count: int32 [32], P('dp'), parts along dimension 0, may hold values from 1 to 6
- vis_len: int32 [32, 6], P('dp'), parts along dimension 0, may hold values from 1 to 128, as said below
Outputs:
- attention: bfloat16 [4096, 8192], P(('dp', 'ctx'), 'head'), parts along dimension 0
- grad_query: bfloat16 [4096, 8192], P(('dp', 'ctx'), 'head'), parts along dimension 0
- grad_key: bfloat16 [4096, 1024], P(('dp', 'ctx'), 'head'), parts along dimension 0
- grad_value: bfloat16 [4096, 1024], P(('dp', 'ctx'), 'head'), parts along dimension 0
The draws below stay inside these ranges and needn't reach their ends.
There are 4 independent parts, one for each index of `dp`. The reference program is written for one: setup_inputs(seed, part) draws one part's arguments, and reference() takes and returns one part's arrays. A program takes and returns all parts, laid end to end along the dimension named above; each array names one. Nothing has to cross between parts.
Inputs may be any that keep to these rules, and one draw needn't show every extreme that they name: `vis_blocks`: slot 0 of row b is b itself; live slots 1 to vis_count[b] - 1 hold distinct blocks before b; slots at or past vis_count[b] hold b. Over the live slots of the 4 rows of one group of 4 consecutive query blocks, at most 2 distinct blocks of any other such group appear. `vis_len`: slot 0 and slots at or past vis_count hold 128.
All inputs are finite; a program needn't handle non-finite values.
Results may differ from the reference program's by a relative error of at most 0.012.
Values may be sent and summed in bfloat16 or wider, within the bound.
No kernel may reach another device: no remote copies, remote signals or barrier semaphores. Data moves between devices by JAX's collectives and lax.ppermute only.
A program may use at most 128 MiB of HBM per device.

```python
import math
import jax
import jax.numpy as jnp
from jax import lax

HEAD_SIZE = 128
QUERY_HEADS = 64
KEY_VALUE_HEADS = 8
MASK_BLOCK_SIZE = 128
VIS = 6
CAP = 2
TOK_DEV = 512
BPD = 4
SEQUENCE_TOKENS = 1024
NB = 8


def tree_lists(key):
    group_count = NB // BPD
    key_pick = jax.random.fold_in(key, 11)
    key_order = jax.random.fold_in(key, 13)
    key_length = jax.random.fold_in(key, 14)
    key_last = jax.random.fold_in(key, 15)
    key_deal = jax.random.fold_in(key, 16)
    key_limit = jax.random.fold_in(key, 17)
    local_index = jnp.arange(BPD, dtype=jnp.int32)
    pick_score = jax.random.randint(key_pick, (group_count, group_count, BPD), 0, 1 << 20) * BPD + local_index
    unused_vals, picked = lax.top_k(pick_score, CAP)
    offered = jnp.any(picked[:, :, :, None] == local_index[None, None, None, :], axis=2)
    offered = offered.reshape(group_count, NB)
    block_index = jnp.arange(NB, dtype=jnp.int32)
    group_index = jnp.arange(group_count, dtype=jnp.int32)
    home_group = block_index // BPD
    remote_ok = offered & (home_group[None, :] < group_index[:, None])
    deal_width = BPD * (VIS - 1)
    order_score = jax.random.randint(key_order, (group_count, NB), 0, 1 << 20) * NB + block_index[None, :]
    order_score = jnp.where(remote_ok, order_score, -1)
    padded = jnp.concatenate([order_score, jnp.full((group_count, deal_width), -1, jnp.int32)], axis=1)
    top_vals, chosen = lax.top_k(padded, deal_width)
    valid = (top_vals >= 0).astype(jnp.int32)
    chosen = chosen.astype(jnp.int32)
    deal_index = jnp.arange(deal_width, dtype=jnp.int32)
    deal_score = jax.random.randint(key_deal, (group_count, deal_width), 0, 1 << 20) * deal_width + deal_index[None, :]
    deal_order = jnp.argsort(deal_score, axis=1, stable=True)
    chosen = jnp.take_along_axis(chosen, deal_order, axis=1)
    valid = jnp.take_along_axis(valid, deal_order, axis=1)
    chosen = jnp.transpose(chosen.reshape(group_count, VIS - 1, BPD), (0, 2, 1)).reshape(NB, VIS - 1)
    valid = jnp.transpose(valid.reshape(group_count, VIS - 1, BPD), (0, 2, 1)).reshape(NB, VIS - 1)
    prior_step = jnp.arange(1, BPD, dtype=jnp.int32)
    prior_blocks = block_index[:, None] - prior_step[None, :]
    prior_valid = (prior_step[None, :] <= (block_index % BPD)[:, None]).astype(jnp.int32)
    prior_blocks = jnp.where(prior_valid > 0, prior_blocks, block_index[:, None]).astype(jnp.int32)
    cand_blocks = jnp.concatenate([chosen, prior_blocks], axis=1)
    cand_valid = jnp.concatenate([valid, prior_valid], axis=1)
    packing = jnp.argsort(1 - cand_valid, axis=1, stable=True)
    chosen = jnp.take_along_axis(cand_blocks, packing, axis=1)[:, :VIS - 1]
    valid = jnp.take_along_axis(cand_valid, packing, axis=1)[:, :VIS - 1]
    limit = jax.random.randint(key_limit, (NB,), 1, VIS + 1).astype(jnp.int32)
    live_count = jnp.minimum(1 + jnp.sum(valid, axis=1), limit).astype(jnp.int32)
    slot_index = jnp.arange(VIS, dtype=jnp.int32)
    listed = jnp.concatenate([block_index[:, None], chosen], axis=1)
    blocks = jnp.where(slot_index[None, :] < live_count[:, None], listed, block_index[:, None])
    last_home = home_group == group_count - 1
    allowed_last = (block_index < NB - 1) & (last_home | offered[group_count - 1])
    last_score = jax.random.randint(key_last, (NB,), 0, 1 << 20) * NB + block_index
    last_score = jnp.where(allowed_last, last_score, -1)
    unused_last, last_pick = lax.top_k(last_score, VIS - 1)
    last_row = jnp.concatenate([jnp.array([NB - 1], jnp.int32), last_pick.astype(jnp.int32)])
    blocks = blocks.at[NB - 1].set(last_row)
    live_count = live_count.at[NB - 1].set(VIS)
    raw_lengths = jax.random.randint(key_length, (NB, VIS), 1, 2 * MASK_BLOCK_SIZE)
    lengths = jnp.minimum(raw_lengths, MASK_BLOCK_SIZE)
    live_other = (slot_index[None, :] >= 1) & (slot_index[None, :] < live_count[:, None])
    lengths = jnp.where(live_other, lengths, MASK_BLOCK_SIZE).astype(jnp.int32)
    return (blocks.astype(jnp.int32), live_count.astype(jnp.int32), lengths)


def draw_vis_blocks(key, part):
    return tree_lists(key)[0]


def draw_vis_count(key, part):
    return tree_lists(key)[1]


def draw_vis_len(key, part):
    return tree_lists(key)[2]


def rows_per_head(key, total_head_count, member):
    total_row_count = SEQUENCE_TOKENS
    own_key = jax.random.fold_in(key, 100 + member)
    values_drawn = jax.random.truncated_normal(own_key, -6.0, 6.0, (total_row_count, total_head_count, HEAD_SIZE), jnp.float32)
    return values_drawn.reshape(total_row_count, total_head_count * HEAD_SIZE)


def draw_query_states(key, part):
    return rows_per_head(key, QUERY_HEADS, 0).astype(jnp.bfloat16)


def draw_key_states(key, part):
    return rows_per_head(key, KEY_VALUE_HEADS, 1).astype(jnp.bfloat16)


def shard_levels(stream_key, shape, cuts, low, high):
    def one(dim, shards_of):
        heights = jax.random.uniform(jax.random.fold_in(jax.random.fold_in(stream_key, 6), dim), (shards_of,), jnp.float32, low / len(cuts), high / len(cuts))
        return jnp.repeat(jnp.exp(heights), shape[dim] // shards_of).reshape((-1,) + (1,) * (len(shape) - dim - 1))

    loudness = one(*cuts[0])
    for cut in cuts[1:]:
        loudness = loudness * one(*cut)
    return loudness


def noise(rng, shape, spread, most, cuts=(), kind=jnp.bfloat16):
    factor_of = shard_levels(rng, shape, cuts, -0.22, 0.18) if cuts else 1.0
    values = jax.random.normal(rng, shape, jnp.float32) * spread * factor_of
    return jnp.minimum(jnp.maximum(values, -most), most).astype(kind)


def setup_inputs(seed: int = 0, part: int = 0) -> dict:
    key_list = jax.random.split(jax.random.key(seed), 8)
    own_keys = jax.random.split(jax.random.fold_in(key_list[7], part), 8)
    return {
        "query_states": draw_query_states(jax.random.fold_in(jax.random.fold_in(key_list[7], part), 71), part),
        "key_states": draw_key_states(jax.random.fold_in(jax.random.fold_in(key_list[7], part), 71), part),
        "value_state_rows": noise(own_keys[2], (SEQUENCE_TOKENS, KEY_VALUE_HEADS * HEAD_SIZE), 1.0, 6.0, ((0, 2), (1, 4))),
        "grad_out": noise(own_keys[3], (SEQUENCE_TOKENS, QUERY_HEADS * HEAD_SIZE), 1.0, 6.0, ((0, 2), (1, 4))),
        "vis_blocks": draw_vis_blocks(jax.random.fold_in(jax.random.fold_in(key_list[7], part), 71), part),
        "vis_count": draw_vis_count(jax.random.fold_in(jax.random.fold_in(key_list[7], part), 71), part),
        "vis_len": draw_vis_len(jax.random.fold_in(jax.random.fold_in(key_list[7], part), 71), part),
    }


masked_score = -1e+30

def to_bf16(array):
    return lax.optimization_barrier(array.astype(jnp.bfloat16)).astype(jnp.float32)

def attend(query_block_rows, gradient_block_rows, key_value_slots, block_id, row_blocks, row_count, row_lens):
    inv_root = 1.0 / math.sqrt(HEAD_SIZE)
    key_value_width = KEY_VALUE_HEADS * HEAD_SIZE
    group_width_count = QUERY_HEADS // KEY_VALUE_HEADS
    total_slot_count = key_value_slots.shape[0]
    query_rows = query_block_rows.astype(jnp.float32).reshape(MASK_BLOCK_SIZE, KEY_VALUE_HEADS, group_width_count, HEAD_SIZE)
    output_gradients = gradient_block_rows.astype(jnp.float32).reshape(MASK_BLOCK_SIZE, KEY_VALUE_HEADS, group_width_count, HEAD_SIZE)
    key_portion = key_value_slots[:, :, :key_value_width].astype(jnp.float32).reshape(total_slot_count, MASK_BLOCK_SIZE, KEY_VALUE_HEADS, HEAD_SIZE)
    value_portion = key_value_slots[:, :, key_value_width:].astype(jnp.float32).reshape(total_slot_count, MASK_BLOCK_SIZE, KEY_VALUE_HEADS, HEAD_SIZE)
    query_pos = jnp.arange(MASK_BLOCK_SIZE, dtype=jnp.int32)[:, None, None]
    key_pos = jnp.arange(MASK_BLOCK_SIZE, dtype=jnp.int32)[None, None, :]
    slot_pos = jnp.arange(total_slot_count, dtype=jnp.int32)[None, :, None]
    visible = (slot_pos < row_count) & (key_pos < row_lens[None, :, None])
    visible = visible & ((row_blocks[None, :, None] != block_id) | (key_pos <= query_pos))
    scores = jnp.einsum('qgrd,vkgd->grqvk', query_rows, key_portion) * inv_root
    row_max = lax.optimization_barrier(jnp.max(jnp.where(visible, scores, masked_score), axis=(3, 4), keepdims=True))
    weights = jnp.exp(jnp.where(visible, scores - row_max, masked_score))
    soft_probs = weights / lax.optimization_barrier(jnp.sum(weights, axis=(3, 4), keepdims=True))
    probs_low = to_bf16(soft_probs)
    attention = jnp.einsum('grqvk,vkgd->qgrd', probs_low, value_portion).astype(jnp.bfloat16).reshape(MASK_BLOCK_SIZE, QUERY_HEADS * HEAD_SIZE)
    dprobs = jnp.einsum('qgrd,vkgd->grqvk', output_gradients, value_portion)
    row_delta = lax.optimization_barrier(jnp.sum(soft_probs * dprobs, axis=(3, 4), keepdims=True))
    dscores = to_bf16(soft_probs * (dprobs - row_delta) * inv_root)
    grad_query = jnp.einsum('grqvk,vkgd->qgrd', dscores, key_portion).astype(jnp.bfloat16).reshape(MASK_BLOCK_SIZE, QUERY_HEADS * HEAD_SIZE)
    grad_keys = jnp.einsum('grqvk,qgrd->vkgd', dscores, query_rows).reshape(total_slot_count, MASK_BLOCK_SIZE, key_value_width)
    grad_values = jnp.einsum('grqvk,qgrd->vkgd', probs_low, output_gradients).reshape(total_slot_count, MASK_BLOCK_SIZE, key_value_width)
    return (attention, grad_query, jnp.concatenate([grad_keys, grad_values], axis=2))

def reference(query_states, key_states, value_state_rows, grad_out, vis_blocks, vis_count, vis_len):
    key_value_width = KEY_VALUE_HEADS * HEAD_SIZE
    heads_each_group = TOK_DEV // MASK_BLOCK_SIZE
    group_total = NB // heads_each_group
    kv_blocks = jnp.concatenate([key_states, value_state_rows], axis=1).reshape(NB, MASK_BLOCK_SIZE, 2 * key_value_width)
    query_groups = query_states.reshape(group_total, heads_each_group, MASK_BLOCK_SIZE, QUERY_HEADS * HEAD_SIZE)
    grad_groups = grad_out.reshape(group_total, heads_each_group, MASK_BLOCK_SIZE, QUERY_HEADS * HEAD_SIZE)
    block_ids = jnp.arange(NB, dtype=jnp.int32).reshape(group_total, heads_each_group)
    block_lists = vis_blocks.reshape(group_total, heads_each_group, VIS)
    count_lists = vis_count.reshape(group_total, heads_each_group)
    length_lists = vis_len.reshape(group_total, heads_each_group, VIS)

    def group_step(carried, pieces):
        query_part, grad_part, ids_part, blocks_part, counts_part, lengths_part = pieces

        def block_step(inner):
            query_block_rows, gradient_block_rows, block_id, row_blocks, row_count, row_lens = inner
            return attend(query_block_rows, gradient_block_rows, kv_blocks[row_blocks], block_id, row_blocks, row_count, row_lens)
        attention, grad_query, slot_grads = lax.map(block_step, (query_part, grad_part, ids_part, blocks_part, counts_part, lengths_part))
        partial_sum = jnp.zeros((NB, MASK_BLOCK_SIZE, 2 * key_value_width), jnp.float32).at[blocks_part.reshape(-1)].add(slot_grads.reshape(heads_each_group * VIS, MASK_BLOCK_SIZE, 2 * key_value_width))
        return (carried + to_bf16(partial_sum), (attention, grad_query))
    summed, (attention, grad_query) = lax.scan(group_step, jnp.zeros((NB, MASK_BLOCK_SIZE, 2 * key_value_width), jnp.float32), (query_groups, grad_groups, block_ids, block_lists, count_lists, length_lists))
    summed = summed.reshape(SEQUENCE_TOKENS, 2 * key_value_width)
    return (attention.reshape(SEQUENCE_TOKENS, QUERY_HEADS * HEAD_SIZE), grad_query.reshape(SEQUENCE_TOKENS, QUERY_HEADS * HEAD_SIZE), summed[:, :key_value_width].astype(jnp.bfloat16), summed[:, key_value_width:].astype(jnp.bfloat16))
```

```python
import functools
import math

import jax
import jax.numpy as jnp
from jax import lax
from jax.experimental import pallas as pl
from jax.experimental.pallas import tpu as pltpu
from jax.sharding import PartitionSpec as P

HEAD_SIZE = 128
BLOCK = 128
CAP = 2
CHUNK = 2
MASKED = -1e30
INV_ROOT = 1.0 / math.sqrt(HEAD_SIZE)
EXP2_SCALE = INV_ROOT * math.log2(math.e)
SMALL_VMEM = 8 * 1024 * 1024
LARGE_VMEM = 16 * 1024 * 1024


def dot(a, b, contract):
    return lax.dot_general(a, b, (contract, ((), ())), preferred_element_type=jnp.float32)


def split(block, per_shard):
    if per_shard & (per_shard - 1) == 0:
        return block >> (per_shard.bit_length() - 1), block & (per_shard - 1)
    return lax.div(block, jnp.int32(per_shard)), lax.rem(block, jnp.int32(per_shard))


def rank_of(bits, index):
    below = bits & ((jnp.int32(1) << index) - 1)
    return jnp.where(below != 0, 1, 0).astype(jnp.int32)


def plan_width(vis):
    return 2 * vis + 1


def plan_size(ctx_size, per_shard, vis):
    return 2 * per_shard * plan_width(vis) + ctx_size - 1


def reader_bits(ctx_size, per_shard, vis):
    return 2 * per_shard * plan_width(vis)


def pack_kernel(
    ctx_size, per_shard, vis, blocks_ref, count_ref, lens_ref, k_ref, v_ref, out_ref, plan_ref, bits_ref, sem
):
    me = lax.axis_index("ctx")
    bits_at = reader_bits(ctx_size, per_shard, vis)

    def each_copy(act):
        for shift in range(1, ctx_size):
            bits = plan_ref[bits_at + shift - 1]
            for index in range(per_shard):

                @pl.when((bits >> index) & 1 == 1)
                def _():
                    rows = pl.ds(index * BLOCK, BLOCK)
                    to = pl.ds(pl.multiple_of(rank_of(bits, jnp.int32(index)) * BLOCK, BLOCK), BLOCK)
                    for part, ref in enumerate((k_ref, v_ref)):
                        act(
                            pltpu.make_async_copy(
                                ref.at[rows, :], out_ref.at[part, shift - 1, to, :], sem.at[shift - 1, index, part]
                            )
                        )

    for shift in range(1, ctx_size):
        reader = me + shift
        plan_ref[bits_at + shift - 1] = jnp.int32(0)

        @pl.when(reader < ctx_size)
        def _():
            bits = jnp.int32(0)
            for row in range(per_shard):
                at = reader * per_shard + row
                count = count_ref[at]
                for slot in range(1, vis):
                    owner, index = split(blocks_ref[at, slot], per_shard)
                    bits = bits | jnp.where((slot < count) & (owner == me), jnp.int32(1) << index, 0)
            plan_ref[bits_at + shift - 1] = bits

    each_copy(lambda copy: copy.start())
    for row in range(per_shard):
        at = me * per_shard + row
        count = count_ref[at]
        near_at = row * plan_width(vis)
        near = jnp.int32(0)
        for slot in range(vis):
            owner, index = split(blocks_ref[at, slot], per_shard)
            plan_ref[near_at + 1 + near] = index
            plan_ref[near_at + 1 + vis + near] = lens_ref[at, slot]
            near = near + ((slot < count) & (owner == me)).astype(jnp.int32)
        plan_ref[near_at] = near
        plan_ref[(per_shard + row) * plan_width(vis)] = jnp.int32(0)

    @pl.when(me > 0)
    def _():
        for owner in range(ctx_size):
            bits_ref[owner] = jnp.int32(0)
        for row in range(per_shard):
            at = me * per_shard + row
            count = count_ref[at]
            for slot in range(1, vis):
                owner, index = split(blocks_ref[at, slot], per_shard)
                bits_ref[owner] = bits_ref[owner] | jnp.where(slot < count, jnp.int32(1) << index, 0)
        for row in range(per_shard):
            at = me * per_shard + row
            count = count_ref[at]
            far_at = (per_shard + row) * plan_width(vis)
            far = jnp.int32(0)
            for slot in range(1, vis):
                owner, index = split(blocks_ref[at, slot], per_shard)
                plan_ref[far_at + 1 + far] = CAP * (me - owner - 1) + rank_of(bits_ref[owner], index)
                plan_ref[far_at + 1 + vis + far] = lens_ref[at, slot]
                far = far + ((slot < count) & (owner != me)).astype(jnp.int32)
            plan_ref[far_at] = far

    each_copy(lambda copy: copy.wait())


def add_kernel(ctx_size, per_shard, vis, plan_ref, own_ref, recv_ref, dk_ref, dv_ref, gk_ref, gv_ref, total_ref, sem):
    del dk_ref, dv_ref
    bits_at = reader_bits(ctx_size, per_shard, vis)
    every = jnp.int32(0)
    for shift in range(1, ctx_size):
        every = every | plan_ref[bits_at + shift - 1]

    def each_block(act):
        for index in range(per_shard):

            @pl.when((every >> index) & 1 == 1)
            def _():
                rows = pl.ds(index * BLOCK, BLOCK)
                for part, dst in enumerate((gk_ref, gv_ref)):
                    act(
                        index, part, rows,
                        pltpu.make_async_copy(total_ref.at[part, rows, :], dst.at[rows, :], sem.at[part, index]),
                    )

    def add(index, part, rows, write):
        def step(s, acc):
            bits = plan_ref[bits_at + s]
            use = (bits >> index) & 1
            to = pl.multiple_of(rank_of(bits, jnp.int32(index)) * BLOCK, BLOCK)
            got = recv_ref[part, s, pl.ds(to, BLOCK), :].astype(jnp.float32)
            return acc + jnp.where(use == 1, got, 0.0)

        total = lax.fori_loop(0, ctx_size - 1, step, own_ref[part, rows, :].astype(jnp.float32))
        total_ref[part, rows, :] = total.astype(jnp.bfloat16)
        write.start()

    each_block(add)
    each_block(lambda index, part, rows, write: write.wait())


def both(first, then):
    def stage(i):
        first(i)
        then(i)

    return stage


def skewed(parts, stages):
    for tick in range(parts + len(stages) - 1):
        for k in reversed(range(len(stages))):
            if 0 <= tick - k < parts:
                stages[k](tick - k)


def rows_of_heads(ref, rows, lanes):
    return jnp.concatenate([ref[rows, l] for l in lanes], axis=0)


def store_heads(ref, rows, lanes, value):
    for i, l in enumerate(lanes):
        ref[rows, l] = value[i * BLOCK : (i + 1) * BLOCK]


def hide(masks, scores):
    return jnp.concatenate(
        [jnp.where(m, scores[:, i * BLOCK : (i + 1) * BLOCK], MASKED) for i, m in enumerate(masks)], axis=1
    )


def head_lanes(width):
    parts = width // (CHUNK * HEAD_SIZE)
    return [[pl.ds((CHUNK * c + i) * HEAD_SIZE, HEAD_SIZE) for i in range(CHUNK)] for c in range(parts)]


def chunk_rows(c):
    return pl.ds(c * CHUNK * BLOCK, CHUNK * BLOCK)


def table_rows(ref, g, pos):
    lanes = pl.ds(g * HEAD_SIZE, HEAD_SIZE)
    return jnp.concatenate([ref[pl.ds(pl.multiple_of(p * BLOCK, BLOCK), BLOCK), lanes] for p in pos], axis=0)


def with_ones(values):
    return jnp.concatenate([values, jnp.ones_like(values)], axis=1)


def table_lanes(ref, g, pos):
    return jnp.concatenate([ref[g, p] for p in pos], axis=1)


def accumulate(acc, g, pos, total):
    for i, p in enumerate(pos):
        acc[g, p] += total[:, i * BLOCK : (i + 1) * BLOCK]


def add_to(total, key, value):
    total[key] = total[key] + value if key in total else value


def iotas(chunk):
    shape = (chunk * BLOCK, BLOCK)
    return lax.broadcasted_iota(jnp.int32, shape, 0) % BLOCK, lax.broadcasted_iota(jnp.int32, shape, 1)


def far_masks(chunk, lens):
    _, key_at = iotas(chunk)
    return [key_at < n for n in lens]


def hidden_bias(masks):
    return jnp.concatenate([jnp.where(m, 0.0, MASKED) for m in masks], axis=1).astype(jnp.bfloat16)


def near_lengths(ctx_size, per_shard, vis, blocks_ref, count_ref, lens_ref):
    me = lax.axis_index("ctx")
    lengths = []
    for row in range(per_shard):
        at = me * per_shard + row
        count = count_ref[at]
        slots = [(blocks_ref[at, s], lens_ref[at, s], s < count) for s in range(1, vis)] if row else []
        of_row = []
        for earlier in range(row):
            length = jnp.int32(0)
            for block, visible, live in slots:
                length = length + jnp.where(live & (block == me * per_shard + earlier), visible, 0)
            of_row.append(length)
        lengths.append(of_row)
    return lengths


def near_masks(chunk, lengths):
    query_at, key_at = iotas(chunk)
    return [key_at < n for n in lengths] + [key_at <= query_at]


def block_rows(row):
    return pl.ds(row * BLOCK, BLOCK)


def forward_kernel(
    ctx_size, per_shard, vis, blocks_ref, count_ref, lens_ref, q_ref, k_ref, v_ref, part_ref, top_ref, norm_ref, p_ref
):
    kv_heads = k_ref.shape[1] // HEAD_SIZE
    lanes = head_lanes(q_ref.shape[1])
    parts = len(lanes)
    lengths = near_lengths(ctx_size, per_shard, vis, blocks_ref, count_ref, lens_ref)
    biases = [hidden_bias(near_masks(1, of_row)) for of_row in lengths]
    query_at, lane_at = iotas(CHUNK)
    which = jnp.where(query_at == lane_at, 1.0, 0.0).astype(jnp.bfloat16)
    heads_at = [pl.ds(g * HEAD_SIZE, HEAD_SIZE) for g in range(kv_heads)]
    k_t = [k_ref[:, at].T for at in heads_at]
    k_bias = [[jnp.concatenate([x[:, : bias.shape[1]], bias], axis=0) for x in k_t] for bias in biases]
    v_one = [with_ones(v_ref[:, at]) for at in heads_at]
    chunks = [(row, c, c * kv_heads // parts) for row in range(per_shard) for c in range(parts)]
    scores, weights, summed = ([None] * len(chunks) for _ in range(3))

    def stage_scores(i):
        row, c, g = chunks[i]
        q = rows_of_heads(q_ref, block_rows(row), lanes[c])
        scores[i] = dot(jnp.concatenate([q, which], axis=1), k_bias[row][g], ((1,), (0,)))

    def stage_weights(i):
        row, c, g = chunks[i]
        seen = scores[i]
        top = jnp.ceil(jnp.max(seen, axis=1, keepdims=True) * EXP2_SCALE)
        weights[i] = jnp.exp2(seen * EXP2_SCALE - top).astype(jnp.bfloat16)
        p_ref[row, chunk_rows(c), pl.ds(0, (row + 1) * BLOCK)] = weights[i]
        store_heads(top_ref, block_rows(row), lanes[c], jnp.broadcast_to(top, (CHUNK * BLOCK, HEAD_SIZE)))

    def stage_summed(i):
        row, c, g = chunks[i]
        summed[i] = dot(weights[i], v_one[g][: (row + 1) * BLOCK], ((1,), (0,)))

    def stage_out(i):
        row, c, g = chunks[i]
        store_heads(part_ref, block_rows(row), lanes[c], summed[i][:, :HEAD_SIZE])
        store_heads(norm_ref, block_rows(row), lanes[c], summed[i][:, HEAD_SIZE:])

    skewed(len(chunks), [stage_scores, stage_weights, stage_summed, stage_out])


def backward_kernel(
    ctx_size, per_shard, vis, q_ref, go_ref, dq_far_ref, delta_ref, p_ref, k_ref, v_ref, att_ref, *rest
):
    own_ref, o_ref, dq_ref, dk_ref, dv_ref, acc_k, acc_v, dq_rows, sem = rest[-9:]
    kv_heads = k_ref.shape[1] // HEAD_SIZE
    lanes = head_lanes(q_ref.shape[1])
    parts = len(lanes)
    heads_at = [pl.ds(g * HEAD_SIZE, HEAD_SIZE) for g in range(kv_heads)]
    copies = [pltpu.make_async_copy(att_ref, o_ref, sem.at[0])]
    copies[0].start()
    v_t = [v_ref[:, at].T for at in heads_at]
    order = list(reversed(range(per_shard)))
    chunks = [(row, c, c * kv_heads // parts) for row in order for c in range(parts)]
    go, dprobs, weights, dscores = ([None] * len(chunks) for _ in range(4))
    total_v, total_k = {}, {}

    def stage_dprobs(i):
        row, c, g = chunks[i]
        go[i] = rows_of_heads(go_ref, block_rows(row), lanes[c])
        dprobs[i] = dot(go[i], v_t[g][:, : (row + 1) * BLOCK], ((1,), (0,)))

    def stage_dscores(i):
        row, c, g = chunks[i]
        delta = repeat(rows_of_heads(delta_ref, block_rows(row), lanes[c]), row + 1)
        weights[i] = p_ref[row, chunk_rows(c), pl.ds(0, (row + 1) * BLOCK)]
        dscores[i] = weights[i] * (dprobs[i] - delta).astype(jnp.bfloat16)

    def stage_grads(i):
        row, c, g = chunks[i]
        dq = dot(dscores[i], k_ref[pl.ds(0, (row + 1) * BLOCK), heads_at[g]], ((1,), (0,)))
        dq = dq + rows_of_heads(dq_far_ref, block_rows(row), lanes[c])
        store_heads(dq_rows, block_rows(row), lanes[c], (dq * INV_ROOT).astype(jnp.bfloat16))
        add_to(total_v, (row, g), dot(go[i], weights[i], ((0,), (0,))))
        add_to(total_k, (row, g), dot(rows_of_heads(q_ref, block_rows(row), lanes[c]), dscores[i], ((0,), (0,))))
        if (c + 1) * kv_heads // parts == g + 1:
            settle(row, g)
        if c == parts - 1:
            copy = pltpu.make_async_copy(
                dq_rows.at[block_rows(row), :], dq_ref.at[block_rows(row), :], sem.at[1 + row]
            )
            copy.start()
            copies.append(copy)

    def settle(row, g):
        for total, acc, part, scale in ((total_k, acc_k, 0, INV_ROOT), (total_v, acc_v, 1, None)):
            value = total[row, g]
            if row < per_shard - 1:
                value = value + acc[g, :, pl.ds(0, (row + 1) * BLOCK)]
            if row:
                acc[g, :, pl.ds(0, row * BLOCK)] = value[:, : row * BLOCK]
            done = value[:, row * BLOCK :]
            done = (done if scale is None else done * scale).astype(jnp.bfloat16).T
            own_ref[part, block_rows(row), heads_at[g]] = done

    skewed(len(chunks), [stage_dprobs, stage_dscores, stage_grads])
    for part, dst in enumerate((dk_ref, dv_ref)):
        copy = pltpu.make_async_copy(own_ref.at[part], dst, sem.at[1 + per_shard + part])
        copy.start()
        copies.append(copy)
    for copy in copies:
        copy.wait()


def finish(rows, lanes, go_ref, out, inv_norm, near, o_ref, go_near_ref, delta_ref):
    store_heads(o_ref, rows, lanes, out.astype(jnp.bfloat16))
    scaled = (rows_of_heads(go_ref, rows, lanes).astype(jnp.float32) * inv_norm).astype(jnp.bfloat16)
    exact = scaled.astype(jnp.float32)
    delta = jnp.sum(exact * out, axis=1, keepdims=True)
    if near is None:
        store_heads(go_near_ref, rows, lanes, scaled)
        store_heads(delta_ref, rows, lanes, jnp.broadcast_to(delta, out.shape))
    else:
        store_heads(go_near_ref, rows, lanes, (exact * near).astype(jnp.bfloat16))
        store_heads(delta_ref, rows, lanes, delta * near)
    return scaled, delta


def only_local(rows, lanes, go_ref, part_ref, norm_ref, o_ref, go_near_ref, delta_ref):
    for of in lanes:
        inv_norm = 1.0 / rows_of_heads(norm_ref, rows, of)
        out = rows_of_heads(part_ref, rows, of) * inv_norm
        finish(rows, of, go_ref, out, inv_norm, None, o_ref, go_near_ref, delta_ref)


def repeat(value, times):
    return jnp.concatenate([value] * times, axis=1)


def with_far(
    slots, kv_heads, rows, q_ref, go_ref, part_ref, top_ref, norm_ref, far_ref, o_ref, dq_ref, go_near_ref, delta_ref,
    kt_t, vt_t, acc_k, acc_v, pos, lens,
):
    lanes = head_lanes(q_ref.shape[1])
    parts = len(lanes)
    kv = [c * kv_heads // parts for c in range(parts)]
    masks = far_masks(CHUNK, lens)
    k_cat = [table_rows(far_ref.at[0], g, pos) for g in range(kv_heads)]
    v_one = [with_ones(table_rows(far_ref.at[1], g, pos)) for g in range(kv_heads)]
    k_cat_t = [table_lanes(kt_t, g, pos) for g in range(kv_heads)]
    v_cat_t = [table_lanes(vt_t, g, pos) for g in range(kv_heads)]
    q, scores, top, near, weights, summed, scaled, delta, dprobs, dscores = ([None] * parts for _ in range(10))
    total_v, total_k = {}, {}

    def stage_scores(c):
        q[c] = rows_of_heads(q_ref, rows, lanes[c])
        scores[c] = dot(q[c], k_cat_t[kv[c]], ((1,), (0,)))

    def stage_weights(c):
        seen = hide(masks, scores[c])
        top_near = rows_of_heads(top_ref, rows, lanes[c])
        top[c] = jnp.maximum(jnp.ceil(jnp.max(seen, axis=1, keepdims=True) * EXP2_SCALE), top_near)
        near[c] = jnp.exp2(top_near - top[c])
        weights[c] = jnp.exp2(seen * EXP2_SCALE - repeat(top[c], slots)).astype(jnp.bfloat16)

    def stage_summed(c):
        summed[c] = dot(weights[c], v_one[kv[c]], ((1,), (0,)))

    def stage_out(c):
        inv_norm = 1.0 / (near[c] * rows_of_heads(norm_ref, rows, lanes[c]) + summed[c][:, HEAD_SIZE:])
        out = (rows_of_heads(part_ref, rows, lanes[c]) * near[c] + summed[c][:, :HEAD_SIZE]) * inv_norm
        scaled[c], delta[c] = finish(rows, lanes[c], go_ref, out, inv_norm, near[c], o_ref, go_near_ref, delta_ref)

    def stage_dprobs(c):
        dprobs[c] = dot(scaled[c], v_cat_t[kv[c]], ((1,), (0,)))

    def stage_dscores(c):
        dscores[c] = (weights[c] * (dprobs[c] - delta[c]).astype(jnp.bfloat16))

    def stage_grads(c):
        store_heads(dq_ref, rows, lanes[c], dot(dscores[c], k_cat[kv[c]], ((1,), (0,))))
        add_to(total_v, kv[c], dot(scaled[c], weights[c], ((0,), (0,))))
        add_to(total_k, kv[c], dot(q[c], dscores[c], ((0,), (0,))))

    skewed(
        parts,
        [stage_scores, stage_weights, stage_summed, stage_out, stage_dprobs, stage_dscores, stage_grads],
    )
    for g in range(kv_heads):
        accumulate(acc_v, g, pos, total_v[g])
        accumulate(acc_k, g, pos, total_k[g])


def flip_table(src, dst, kv_heads, count):
    for g in range(kv_heads):
        for i in range(count):
            dst[g, i] = src[pl.ds(i * BLOCK, BLOCK), pl.ds(g * HEAD_SIZE, HEAD_SIZE)].T


def flush(acc, dst, kv_heads, count, scale):
    for g in range(kv_heads):
        for i in range(count):
            value = acc[g, i] if scale is None else acc[g, i] * scale
            dst[pl.ds(i * BLOCK, BLOCK), pl.ds(g * HEAD_SIZE, HEAD_SIZE)] = value.astype(jnp.bfloat16).T


def step_rows():
    row = pl.program_id(0)
    return row, pl.ds(pl.multiple_of(row * BLOCK, BLOCK), BLOCK)


def for_slots(plan_ref, at, most, vis, run):
    size = plan_ref[at]
    for slots in range(1, most + 1):

        @pl.when(size == slots)
        def _():
            pos = [plan_ref[at + 1 + slot] for slot in range(slots)]
            lens = [plan_ref[at + 1 + vis + slot] for slot in range(slots)]
            run(slots, pos, lens)


def far_kernel(
    ctx_size, per_shard, vis, plan_ref, q_ref, go_ref, part_ref, top_ref, norm_ref, far_ref,
    o_ref, dq_ref, delta_ref, go_near_ref, dfar_ref, kt_t, vt_t, acc_k, acc_v,
):
    row, rows = step_rows()
    far = CAP * (ctx_size - 1)
    kv_heads = far_ref.shape[2] // HEAD_SIZE
    at = (per_shard + row) * plan_width(vis)

    @pl.when(row == 0)
    def _():
        flip_table(far_ref.at[0], kt_t, kv_heads, far)
        flip_table(far_ref.at[1], vt_t, kv_heads, far)
        acc_k[...] = jnp.zeros_like(acc_k)
        acc_v[...] = jnp.zeros_like(acc_v)

    @pl.when(plan_ref[at] == 0)
    def _():
        only_local(rows, head_lanes(go_ref.shape[1]), go_ref, part_ref, norm_ref, o_ref, go_near_ref, delta_ref)
        dq_ref[rows, :] = jnp.zeros((BLOCK, dq_ref.shape[1]), dq_ref.dtype)

    def run(slots, pos, lens):
        with_far(
            slots, kv_heads, rows, q_ref, go_ref, part_ref, top_ref, norm_ref, far_ref, o_ref, dq_ref, go_near_ref, delta_ref,
            kt_t, vt_t, acc_k, acc_v, pos, lens,
        )

    for_slots(plan_ref, at, min(vis - 1, far), vis, run)

    @pl.when(row == pl.num_programs(0) - 1)
    def _():
        flush(acc_k, dfar_ref.at[0], kv_heads, far, INV_ROOT)
        flush(acc_v, dfar_ref.at[1], kv_heads, far, None)


def far_blocks(per_shard, vis, blocks_ref, count_ref, reader, owner):
    first, second = jnp.int32(per_shard), jnp.int32(-1)
    for row in range(per_shard):
        at = reader * per_shard + row
        count = count_ref[at]
        for slot in range(1, vis):
            of, index = split(blocks_ref[at, slot], per_shard)
            take = (slot < count) & (of == owner)
            first = jnp.minimum(first, jnp.where(take, index, per_shard))
            second = jnp.maximum(second, jnp.where(take, index, -1))
    return jnp.minimum(first, per_shard - 1), jnp.maximum(second, 0), second >= 0


def pack_pair_kernel(per_shard, vis, blocks_ref, count_ref, k_ref, v_ref, *rest):
    *out_refs, wide_ref, sem = rest
    me = lax.axis_index("ctx")

    @pl.when(me == 0)
    def _():
        first, second, _ = far_blocks(per_shard, vis, blocks_ref, count_ref, 1, 0)
        copies = []
        for place, index in enumerate((first, second)):
            rows = pl.ds(pl.multiple_of(index * BLOCK, BLOCK), BLOCK)
            for part, ref in enumerate((k_ref, v_ref)):
                copies.append(
                    pltpu.make_async_copy(
                        ref.at[rows, :], wide_ref.at[part, block_rows(place), :], sem.at[place, part]
                    )
                )
        for copy in copies:
            copy.start()
        for copy in copies:
            copy.wait()
        for g, out_ref in enumerate(out_refs):
            out_ref[:, 0] = wide_ref[:, :, pl.ds(g * HEAD_SIZE, HEAD_SIZE)]


def add_pair_kernel(
    per_shard, vis, blocks_ref, count_ref, own_ref, *rest
):
    *recv_refs, _, _, gk_ref, gv_ref, total_ref, sem = rest

    @pl.when(lax.axis_index("ctx") == 0)
    def _():
        first, second, _ = far_blocks(per_shard, vis, blocks_ref, count_ref, 1, 0)
        same = first == second
        copies = []
        for place, index in enumerate((first, second)):
            rows = pl.ds(pl.multiple_of(index * BLOCK, BLOCK), BLOCK)
            for part, dst in enumerate((gk_ref, gv_ref)):
                for g, recv_ref in enumerate(recv_refs):
                    lanes = pl.ds(g * HEAD_SIZE, HEAD_SIZE)
                    got = [recv_ref[part, 0, block_rows(p), :].astype(jnp.float32) for p in (place, 1 - place)]
                    total = own_ref[part, rows, lanes].astype(jnp.float32) + got[0] + jnp.where(same, got[1], 0.0)
                    total_ref[part, block_rows(place), lanes] = total.astype(jnp.bfloat16)
                copy = pltpu.make_async_copy(
                    total_ref.at[part, block_rows(place), :], dst.at[rows, :], sem.at[place, part]
                )
                copies.append((place, copy))

        def each(act):
            for place, copy in copies:
                if place == 0:
                    act(copy)
                else:
                    pl.when(jnp.logical_not(same))(functools.partial(act, copy))

        each(lambda copy: copy.start())
        each(lambda copy: copy.wait())


def far_pair_kernel(
    per_shard, vis, kv_heads, g, blocks_ref, count_ref, lens_ref, q_ref, go_ref, part_ref, top_ref, norm_ref, far_ref,
    *rest
):
    o_ref, dq_ref, delta_ref, go_near_ref, dfar_ref = rest[-5:]
    me = lax.axis_index("ctx")
    lanes = head_lanes(q_ref.shape[1])
    per_kv = len(lanes) // kv_heads
    lanes = lanes[g * per_kv : (g + 1) * per_kv]
    all_lanes = pl.ds(g * per_kv * CHUNK * HEAD_SIZE, per_kv * CHUNK * HEAD_SIZE)
    first, second, some = far_blocks(per_shard, vis, blocks_ref, count_ref, me, me - 1)

    @pl.when(jnp.logical_not(some))
    def _():
        for row in range(per_shard):
            only_local(block_rows(row), lanes, go_ref, part_ref, norm_ref, o_ref, go_near_ref, delta_ref)
        dq_ref[:, all_lanes] = jnp.zeros((dq_ref.shape[0], all_lanes.size), dq_ref.dtype)
        dfar_ref[...] = jnp.zeros_like(dfar_ref)

    @pl.when(some)
    def _():
        earlier = (me - 1) * per_shard
        masks = []
        for row in range(per_shard):
            at = me * per_shard + row
            count = count_ref[at]
            lens = [jnp.int32(0), jnp.int32(0)]
            for slot in range(1, vis):
                block, visible = blocks_ref[at, slot], lens_ref[at, slot]
                live = slot < count
                lens[0] = lens[0] + jnp.where(live & (block == earlier + first), visible, 0)
                lens[1] = lens[1] + jnp.where(live & (block == earlier + second) & (first != second), visible, 0)
            masks.append(far_masks(CHUNK, lens))
        k, v = far_ref[0], far_ref[1]
        k_t, v_t, v_one = k.T, v.T, with_ones(v)
        chunks = [(row, c) for row in range(per_shard) for c in range(per_kv)]
        q, scores, top, near, weights, summed, scaled, delta, dprobs, dscores = (
            [None] * len(chunks) for _ in range(10)
        )
        total = {}

        def stage_scores(i):
            row, c = chunks[i]
            q[i] = rows_of_heads(q_ref, block_rows(row), lanes[c])
            scores[i] = dot(q[i], k_t, ((1,), (0,)))

        def stage_weights(i):
            row, c = chunks[i]
            seen = hide(masks[row], scores[i])
            top_near = rows_of_heads(top_ref, block_rows(row), lanes[c])
            top[i] = jnp.maximum(jnp.ceil(jnp.max(seen, axis=1, keepdims=True) * EXP2_SCALE), top_near)
            near[i] = jnp.exp2(top_near - top[i])
            weights[i] = jnp.exp2(seen * EXP2_SCALE - repeat(top[i], CAP)).astype(jnp.bfloat16)

        def stage_summed(i):
            summed[i] = dot(weights[i], v_one, ((1,), (0,)))

        def stage_out(i):
            row, c = chunks[i]
            rows = block_rows(row)
            inv_norm = 1.0 / (near[i] * rows_of_heads(norm_ref, rows, lanes[c]) + summed[i][:, HEAD_SIZE:])
            out = (rows_of_heads(part_ref, rows, lanes[c]) * near[i] + summed[i][:, :HEAD_SIZE]) * inv_norm
            scaled[i], delta[i] = finish(rows, lanes[c], go_ref, out, inv_norm, near[i], o_ref, go_near_ref, delta_ref)

        def stage_dprobs(i):
            dprobs[i] = dot(scaled[i], v_t, ((1,), (0,)))

        def stage_dscores(i):
            dscores[i] = weights[i] * (dprobs[i] - delta[i]).astype(jnp.bfloat16)

        def stage_grads(i):
            row, c = chunks[i]
            store_heads(dq_ref, block_rows(row), lanes[c], dot(dscores[i], k, ((1,), (0,))))
            add_to(total, 1, dot(scaled[i], weights[i], ((0,), (0,))))
            add_to(total, 0, dot(q[i], dscores[i], ((0,), (0,))))

        skewed(
            len(chunks),
            [stage_scores, stage_weights, both(stage_summed, stage_out), both(stage_dprobs, stage_dscores), stage_grads],
        )
        dfar_ref[0] = (total[0] * INV_ROOT).astype(jnp.bfloat16).T
        dfar_ref[1] = total[1].astype(jnp.bfloat16).T


def body(ctx_size, query_states, key_states, value_state_rows, grad_out, vis_blocks, vis_count, vis_len):
    tokens, q_width = query_states.shape
    kv_width = key_states.shape[1]
    heads = kv_width // HEAD_SIZE
    per_shard = tokens // BLOCK
    vis = vis_blocks.shape[1]
    far = CAP * (ctx_size - 1)
    smem = pl.BlockSpec(memory_space=pltpu.SMEM)
    vmem = pl.BlockSpec(memory_space=pltpu.VMEM)
    hbm = pl.BlockSpec(memory_space=pltpu.HBM)
    bf16 = jnp.bfloat16
    pin = lambda array: pltpu.with_memory_space_constraint(array, pltpu.HBM)
    pair = ctx_size == 2
    sent_type = jax.ShapeDtypeStruct((2, ctx_size - 1, CAP * BLOCK, kv_width), bf16)
    busy = pl.CostEstimate(flops=10**10, bytes_accessed=2**20, transcendentals=0)
    small = pltpu.CompilerParams(vmem_limit_bytes=SMALL_VMEM)
    if pair:
        sent = pl.pallas_call(
            functools.partial(pack_pair_kernel, per_shard, vis),
            out_shape=[jax.ShapeDtypeStruct((2, 1, CAP * BLOCK, HEAD_SIZE), bf16)] * heads,
            in_specs=[smem, smem, hbm, hbm],
            out_specs=[vmem] * heads,
            scratch_shapes=[pltpu.VMEM((2, CAP * BLOCK, kv_width), bf16), pltpu.SemaphoreType.DMA((CAP, 2))],
            compiler_params=small,
            cost_estimate=busy,
            name="pack",
        )(pin(vis_blocks), pin(vis_count), pin(key_states), pin(value_state_rows))
    else:
        sent, plan = pl.pallas_call(
            functools.partial(pack_kernel, ctx_size, per_shard, vis),
            out_shape=[sent_type, jax.ShapeDtypeStruct((plan_size(ctx_size, per_shard, vis),), jnp.int32)],
            in_specs=[smem, smem, smem, hbm, hbm],
            out_specs=[vmem, smem],
            scratch_shapes=[
                pltpu.SMEM((ctx_size,), jnp.int32),
                pltpu.SemaphoreType.DMA((ctx_size - 1, per_shard, 2)),
            ],
            compiler_params=small,
            cost_estimate=busy,
            name="pack",
        )(pin(vis_blocks), pin(vis_count), pin(vis_len), pin(key_states), pin(value_state_rows))

    def move(array, back):
        parts = []
        for shift in range(1, ctx_size):
            pairs = [(i, i + shift) for i in range(ctx_size - shift)]
            if back:
                pairs = [(b, a) for a, b in pairs]
            parts.append(lax.ppermute(array[:, shift - 1 : shift], "ctx", pairs))
        return parts[0] if len(parts) == 1 else jnp.concatenate(parts, axis=1)

    if pair:
        got = [move(array, False).reshape(2, far * BLOCK, HEAD_SIZE) for array in reversed(sent)][::-1]
    else:
        got = move(sent, False).reshape(2, far * BLOCK, kv_width)
    q_type = jax.ShapeDtypeStruct(query_states.shape, bf16)
    part_type = jax.ShapeDtypeStruct(query_states.shape, jnp.float32)
    kv_type = jax.ShapeDtypeStruct(key_states.shape, bf16)
    weights_type = jax.ShapeDtypeStruct((per_shard, q_width // HEAD_SIZE * BLOCK, per_shard * BLOCK), bf16)
    flipped = lambda n, kind: pltpu.VMEM((heads, n, HEAD_SIZE, BLOCK), kind)
    large = pltpu.CompilerParams(vmem_limit_bytes=LARGE_VMEM + far // 4 * 2**20)
    flops = 2 * tokens * tokens * q_width
    cost = lambda n: pl.CostEstimate(flops=n * flops, bytes_accessed=8 * 2**20, transcendentals=0)
    lists = (pin(vis_blocks), pin(vis_count), pin(vis_len))
    part, top, norm, weights = pl.pallas_call(
        functools.partial(forward_kernel, ctx_size, per_shard, vis),
        out_shape=[part_type] * 3 + [weights_type],
        in_specs=[smem] * 3 + [vmem] * 3,
        out_specs=[vmem] * 4,
        compiler_params=large,
        cost_estimate=pl.CostEstimate(flops=2**20, bytes_accessed=2**20, transcendentals=0),
        name="forward_local",
    )(*lists, query_states, key_states, value_state_rows)
    far_types = [q_type, part_type, part_type, q_type]
    if pair:
        attention, dq_far, delta, go_near = None, part, top, None
        dfar = []
        for g in range(heads):
            before = [] if g == 0 else [attention, go_near]
            attention, dq_far, delta, go_near, array = pl.pallas_call(
                functools.partial(far_pair_kernel, per_shard, vis, heads, g),
                out_shape=far_types + [jax.ShapeDtypeStruct(got[g].shape, bf16)],
                in_specs=[smem] * 3 + [vmem] * (6 + len(before)),
                out_specs=[vmem] * 5,
                input_output_aliases={5: 1, 6: 2} | ({9: 0, 10: 3} if before else {}),
                compiler_params=large,
                cost_estimate=cost(3),
                name="far",
            )(*lists, query_states, grad_out, dq_far, delta, norm, got[g], *before)
            dfar.append(array)
    else:
        attention, dq_far, delta, go_near, dfar = pl.pallas_call(
            functools.partial(far_kernel, ctx_size, per_shard, vis),
            out_shape=far_types + [jax.ShapeDtypeStruct(got.shape, bf16)],
            grid_spec=pltpu.PrefetchScalarGridSpec(
                num_scalar_prefetch=1,
                grid=(per_shard,),
                in_specs=[vmem] * 6,
                out_specs=[vmem] * 5,
                scratch_shapes=[flipped(far, bf16)] * 2 + [flipped(far, jnp.float32)] * 2,
            ),
            input_output_aliases={3: 1, 4: 2},
            compiler_params=large,
            cost_estimate=cost(6),
            name="far",
        )(plan, query_states, grad_out, part, top, norm, got)
    if pair:
        returned = [move(array.reshape(2, 1, CAP * BLOCK, HEAD_SIZE), True) for array in dfar]
    else:
        returned = [move(dfar.reshape(sent.shape), True)]
    earlier = returned[:-1]
    own, attention, grad_query, dk, dv = pl.pallas_call(
        functools.partial(backward_kernel, ctx_size, per_shard, vis),
        out_shape=[jax.ShapeDtypeStruct((2, tokens, kv_width), bf16), q_type, q_type, kv_type, kv_type],
        in_specs=[vmem] * (8 + len(earlier)),
        out_specs=[vmem] + [hbm] * 4,
        scratch_shapes=[pltpu.VMEM((heads, HEAD_SIZE, tokens), jnp.float32)] * 2
        + [pltpu.VMEM(query_states.shape, bf16), pltpu.SemaphoreType.DMA((3 + per_shard,))],
        compiler_params=large,
        cost_estimate=cost(5),
        name="backward_local",
    )(query_states, go_near, dq_far, delta, weights, key_states, value_state_rows, attention, *earlier)
    add, lists = (add_pair_kernel, lists[:2]) if pair else (functools.partial(add_kernel, ctx_size), (plan,))
    grad_key, grad_value = pl.pallas_call(
        functools.partial(add, per_shard, vis),
        out_shape=[kv_type, kv_type],
        in_specs=[smem] * len(lists) + [vmem] * (1 + len(returned)) + [hbm, hbm],
        out_specs=[hbm, hbm],
        scratch_shapes=[
            pltpu.VMEM((2, tokens, kv_width), bf16),
            pltpu.SemaphoreType.DMA((2, per_shard)),
        ],
        input_output_aliases={len(lists) + len(returned) + 1: 0, len(lists) + len(returned) + 2: 1},
        compiler_params=small,
        name="add",
    )(*lists, own, *returned, dk, dv)
    return attention, grad_query, grad_key, grad_value


def solution(mesh):
    rows = P(("dp", "ctx"), "head")
    return jax.shard_map(
        functools.partial(body, mesh.shape["ctx"]),
        mesh=mesh,
        in_specs=(rows, rows, rows, rows, P("dp", None), P("dp"), P("dp", None)),
        out_specs=(rows, rows, rows, rows),
        check_vma=False,
    )
```

```python
import functools
import math

import jax
import jax.numpy as jnp
from jax import lax
from jax.experimental import pallas as pl
from jax.experimental.pallas import tpu as pltpu
from jax.sharding import PartitionSpec as P

HEAD_SIZE = 128
BLOCK = 128
CAP = 2
CHUNK = 2
MASKED = -1e30
INV_ROOT = 1.0 / math.sqrt(HEAD_SIZE)
EXP2_SCALE = INV_ROOT * math.log2(math.e)
SUM_LIMIT = 2.0**96
SMALL_VMEM = 8 * 1024 * 1024
LARGE_VMEM = 14 * 1024 * 1024


def dot(a, b, contract):
    return lax.dot_general(a, b, (contract, ((), ())), preferred_element_type=jnp.float32)


def split(block, per_shard):
    if per_shard & (per_shard - 1) == 0:
        return block >> (per_shard.bit_length() - 1), block & (per_shard - 1)
    return lax.div(block, jnp.int32(per_shard)), lax.rem(block, jnp.int32(per_shard))


def rank_of(bits, index):
    below = bits & ((jnp.int32(1) << index) - 1)
    return jnp.where(below != 0, 1, 0).astype(jnp.int32)


def plan_width(vis):
    return 2 * vis + 1


def plan_size(ctx_size, per_shard, vis):
    return 2 * per_shard * plan_width(vis) + ctx_size - 1


def reader_bits(ctx_size, per_shard, vis):
    return 2 * per_shard * plan_width(vis)


def pack_kernel(
    ctx_size, per_shard, vis, blocks_ref, count_ref, lens_ref, k_ref, v_ref, out_ref, plan_ref, bits_ref, sem
):
    me = lax.axis_index("ctx")
    bits_at = reader_bits(ctx_size, per_shard, vis)

    def each_copy(act):
        for shift in range(1, ctx_size):
            bits = plan_ref[bits_at + shift - 1]
            for index in range(per_shard):

                @pl.when((bits >> index) & 1 == 1)
                def _():
                    rows = pl.ds(index * BLOCK, BLOCK)
                    to = pl.ds(pl.multiple_of(rank_of(bits, jnp.int32(index)) * BLOCK, BLOCK), BLOCK)
                    for part, ref in enumerate((k_ref, v_ref)):
                        act(
                            pltpu.make_async_copy(
                                ref.at[rows, :], out_ref.at[part, shift - 1, to, :], sem.at[shift - 1, index, part]
                            )
                        )

    for shift in range(1, ctx_size):
        reader = me + shift
        plan_ref[bits_at + shift - 1] = jnp.int32(0)

        @pl.when(reader < ctx_size)
        def _():
            bits = jnp.int32(0)
            for row in range(per_shard):
                at = reader * per_shard + row
                count = count_ref[at]
                for slot in range(1, vis):
                    owner, index = split(blocks_ref[at, slot], per_shard)
                    bits = bits | jnp.where((slot < count) & (owner == me), jnp.int32(1) << index, 0)
            plan_ref[bits_at + shift - 1] = bits

    each_copy(lambda copy: copy.start())
    for row in range(per_shard):
        at = me * per_shard + row
        count = count_ref[at]
        near_at = row * plan_width(vis)
        near = jnp.int32(0)
        for slot in range(vis):
            owner, index = split(blocks_ref[at, slot], per_shard)
            plan_ref[near_at + 1 + near] = index
            plan_ref[near_at + 1 + vis + near] = lens_ref[at, slot]
            near = near + ((slot < count) & (owner == me)).astype(jnp.int32)
        plan_ref[near_at] = near
        plan_ref[(per_shard + row) * plan_width(vis)] = jnp.int32(0)

    @pl.when(me > 0)
    def _():
        for owner in range(ctx_size):
            bits_ref[owner] = jnp.int32(0)
        for row in range(per_shard):
            at = me * per_shard + row
            count = count_ref[at]
            for slot in range(1, vis):
                owner, index = split(blocks_ref[at, slot], per_shard)
                bits_ref[owner] = bits_ref[owner] | jnp.where(slot < count, jnp.int32(1) << index, 0)
        for row in range(per_shard):
            at = me * per_shard + row
            count = count_ref[at]
            far_at = (per_shard + row) * plan_width(vis)
            far = jnp.int32(0)
            for slot in range(1, vis):
                owner, index = split(blocks_ref[at, slot], per_shard)
                plan_ref[far_at + 1 + far] = CAP * (me - owner - 1) + rank_of(bits_ref[owner], index)
                plan_ref[far_at + 1 + vis + far] = lens_ref[at, slot]
                far = far + ((slot < count) & (owner != me)).astype(jnp.int32)
            plan_ref[far_at] = far

    each_copy(lambda copy: copy.wait())


def add_kernel(ctx_size, per_shard, vis, plan_ref, own_ref, recv_ref, dk_ref, dv_ref, gk_ref, gv_ref, total_ref, sem):
    del dk_ref, dv_ref
    bits_at = reader_bits(ctx_size, per_shard, vis)
    every = jnp.int32(0)
    for shift in range(1, ctx_size):
        every = every | plan_ref[bits_at + shift - 1]

    def each_block(act):
        for index in range(per_shard):

            @pl.when((every >> index) & 1 == 1)
            def _():
                rows = pl.ds(index * BLOCK, BLOCK)
                for part, dst in enumerate((gk_ref, gv_ref)):
                    act(
                        index, part, rows,
                        pltpu.make_async_copy(total_ref.at[part, rows, :], dst.at[rows, :], sem.at[part, index]),
                    )

    def add(index, part, rows, write):
        def step(s, acc):
            bits = plan_ref[bits_at + s]
            use = (bits >> index) & 1
            to = pl.multiple_of(rank_of(bits, jnp.int32(index)) * BLOCK, BLOCK)
            got = recv_ref[part, s, pl.ds(to, BLOCK), :].astype(jnp.float32)
            return acc + jnp.where(use == 1, got, 0.0)

        total = lax.fori_loop(0, ctx_size - 1, step, own_ref[part, rows, :].astype(jnp.float32))
        total_ref[part, rows, :] = total.astype(jnp.bfloat16)
        write.start()

    each_block(add)
    each_block(lambda index, part, rows, write: write.wait())


def both(first, then):
    def stage(i):
        first(i)
        then(i)

    return stage


def skewed(parts, stages):
    for tick in range(parts + len(stages) - 1):
        for k in reversed(range(len(stages))):
            if 0 <= tick - k < parts:
                stages[k](tick - k)


def rows_of_heads(ref, rows, lanes):
    return jnp.concatenate([ref[rows, l] for l in lanes], axis=0)


def store_heads(ref, rows, lanes, value):
    for i, l in enumerate(lanes):
        ref[rows, l] = value[i * BLOCK : (i + 1) * BLOCK]


def hide(masks, scores):
    return jnp.concatenate(
        [jnp.where(m, scores[:, i * BLOCK : (i + 1) * BLOCK], MASKED) for i, m in enumerate(masks)], axis=1
    )


def head_lanes(width):
    parts = width // (CHUNK * HEAD_SIZE)
    return [[pl.ds((CHUNK * c + i) * HEAD_SIZE, HEAD_SIZE) for i in range(CHUNK)] for c in range(parts)]


def row_lanes(row):
    return pl.ds(row * (row + 1) // 2 * BLOCK, (row + 1) * BLOCK)


def chunk_rows(c):
    return pl.ds(c * CHUNK * BLOCK, CHUNK * BLOCK)


def table_rows(ref, g, pos):
    lanes = pl.ds(g * HEAD_SIZE, HEAD_SIZE)
    return jnp.concatenate([ref[pl.ds(pl.multiple_of(p * BLOCK, BLOCK), BLOCK), lanes] for p in pos], axis=0)


def with_ones(values):
    return jnp.concatenate([values, jnp.ones_like(values)], axis=1)


def table_lanes(ref, g, pos):
    return jnp.concatenate([ref[g, p] for p in pos], axis=1)


def accumulate(acc, g, pos, total):
    for i, p in enumerate(pos):
        acc[g, p] += total[:, i * BLOCK : (i + 1) * BLOCK]


def add_to(total, key, value):
    total[key] = total[key] + value if key in total else value


def iotas(chunk):
    shape = (chunk * BLOCK, BLOCK)
    return lax.broadcasted_iota(jnp.int32, shape, 0) % BLOCK, lax.broadcasted_iota(jnp.int32, shape, 1)


def far_masks(chunk, lens):
    _, key_at = iotas(chunk)
    return [key_at < n for n in lens]


def hidden_bias(masks):
    return jnp.concatenate([jnp.where(m, 0.0, MASKED) for m in masks], axis=1).astype(jnp.bfloat16)


def near_lengths(ctx_size, per_shard, vis, blocks_ref, count_ref, lens_ref):
    me = lax.axis_index("ctx")
    lengths = []
    for row in range(per_shard):
        at = me * per_shard + row
        count = count_ref[at]
        slots = [(blocks_ref[at, s], lens_ref[at, s], s < count) for s in range(1, vis)] if row else []
        of_row = []
        for earlier in range(row):
            length = jnp.int32(0)
            for block, visible, live in slots:
                length = length + jnp.where(live & (block == me * per_shard + earlier), visible, 0)
            of_row.append(length)
        lengths.append(of_row)
    return lengths


def near_masks(chunk, lengths):
    query_at, key_at = iotas(chunk)
    return [key_at < n for n in lengths] + [key_at <= query_at]


def block_rows(row):
    return pl.ds(row * BLOCK, BLOCK)


def chunk_lanes(c):
    at = [pl.multiple_of((CHUNK * c + i) * HEAD_SIZE, HEAD_SIZE) for i in range(CHUNK)]
    return [pl.ds(x, HEAD_SIZE) for x in at]


def forward_kernel(
    ctx_size, per_shard, vis, blocks_ref, count_ref, lens_ref, q_ref, k_ref, v_ref,
    part_ref, top_ref, norm_ref, p_ref, shifted_ref,
):
    kv_heads = k_ref.shape[1] // HEAD_SIZE
    lanes = head_lanes(q_ref.shape[1])
    parts = len(lanes)
    per_kv = parts // kv_heads
    lengths = near_lengths(ctx_size, per_shard, vis, blocks_ref, count_ref, lens_ref)
    biases = [hidden_bias(near_masks(1, of_row)) for of_row in lengths]
    query_at, lane_at = iotas(CHUNK)
    which = jnp.where(query_at == lane_at, 1.0, 0.0).astype(jnp.bfloat16)
    heads_at = [pl.ds(g * HEAD_SIZE, HEAD_SIZE) for g in range(kv_heads)]
    k_t = [k_ref[:, at].T for at in heads_at]
    k_bias = [[jnp.concatenate([x[:, : bias.shape[1]], bias], axis=0) for x in k_t] for bias in biases]
    v_one = [with_ones(v_ref[:, at]) for at in heads_at]
    chunks = [(row, c, c // per_kv) for row in range(per_shard) for c in range(parts)]
    scores, weights, summed = ([None] * len(chunks) for _ in range(3))
    bounds = [None, None]

    def score(row, at, g):
        q = rows_of_heads(q_ref, block_rows(row), at)
        return dot(jnp.concatenate([q, which], axis=1), k_bias[row][g], ((1,), (0,)))

    def stage_scores(i):
        row, c, g = chunks[i]
        scores[i] = score(row, lanes[c], g)

    def stage_weights(i):
        row, c, g = chunks[i]
        weights[i] = jnp.exp2(scores[i] * EXP2_SCALE).astype(jnp.bfloat16)
        p_ref[chunk_rows(c), row_lanes(row)] = weights[i]

    def stage_summed(i):
        row, c, g = chunks[i]
        summed[i] = dot(weights[i], v_one[g][: (row + 1) * BLOCK], ((1,), (0,)))

    def stage_out(i):
        row, c, g = chunks[i]
        norm = summed[i][:, HEAD_SIZE:]
        store_heads(part_ref, block_rows(row), lanes[c], summed[i][:, :HEAD_SIZE])
        store_heads(norm_ref, block_rows(row), lanes[c], norm)
        bounds[0] = norm if i == 0 else jnp.minimum(bounds[0], norm)
        bounds[1] = norm if i == 0 else jnp.maximum(bounds[1], norm)

    skewed(len(chunks), [stage_scores, stage_weights, stage_summed, stage_out])
    good = (jnp.min(bounds[0]) > 1.0 / SUM_LIMIT) & (jnp.max(bounds[1]) < SUM_LIMIT)
    shifted_ref[0] = jnp.where(good, 0, 1).astype(jnp.int32)

    @pl.when(jnp.logical_not(good))
    def _():
        for row in range(per_shard):
            for g in range(kv_heads):

                def step(c, carry):
                    at = chunk_lanes(c)
                    seen = score(row, at, g)
                    top = jnp.ceil(jnp.max(seen, axis=1, keepdims=True) * EXP2_SCALE)
                    low = jnp.exp2(seen * EXP2_SCALE - top).astype(jnp.bfloat16)
                    rows = pl.ds(pl.multiple_of(c * CHUNK * BLOCK, CHUNK * BLOCK), CHUNK * BLOCK)
                    p_ref[rows, row_lanes(row)] = low
                    out = dot(low, v_one[g][: (row + 1) * BLOCK], ((1,), (0,)))
                    store_heads(top_ref, block_rows(row), at, jnp.broadcast_to(top, (CHUNK * BLOCK, HEAD_SIZE)))
                    store_heads(part_ref, block_rows(row), at, out[:, :HEAD_SIZE])
                    store_heads(norm_ref, block_rows(row), at, out[:, HEAD_SIZE:])
                    return carry

                lax.fori_loop(g * per_kv, (g + 1) * per_kv, step, 0)


def backward_kernel(
    ctx_size, per_shard, vis, q_ref, go_ref, dq_far_ref, delta_ref, p_ref, k_ref, v_ref, att_ref, *rest
):
    own_ref, o_ref, dq_ref, dk_ref, dv_ref, acc_k, acc_v, dq_rows, sem = rest[-9:]
    kv_heads = k_ref.shape[1] // HEAD_SIZE
    lanes = head_lanes(q_ref.shape[1])
    parts = len(lanes)
    heads_at = [pl.ds(g * HEAD_SIZE, HEAD_SIZE) for g in range(kv_heads)]
    copies = [pltpu.make_async_copy(att_ref, o_ref, sem.at[0])]
    copies[0].start()
    v_t = [v_ref[:, at].T for at in heads_at]
    order = list(reversed(range(per_shard)))
    chunks = [(row, c, c * kv_heads // parts) for row in order for c in range(parts)]
    go, dprobs, weights, dscores = ([None] * len(chunks) for _ in range(4))
    total_v, total_k = {}, {}

    def stage_dprobs(i):
        row, c, g = chunks[i]
        go[i] = rows_of_heads(go_ref, block_rows(row), lanes[c])
        dprobs[i] = dot(go[i], v_t[g][:, : (row + 1) * BLOCK], ((1,), (0,)))

    def stage_dscores(i):
        row, c, g = chunks[i]
        delta = repeat(rows_of_heads(delta_ref, block_rows(row), lanes[c]), row + 1)
        weights[i] = p_ref[chunk_rows(c), row_lanes(row)]
        dscores[i] = weights[i] * (dprobs[i] - delta).astype(jnp.bfloat16)

    def stage_grads(i):
        row, c, g = chunks[i]
        dq = dot(dscores[i], k_ref[pl.ds(0, (row + 1) * BLOCK), heads_at[g]], ((1,), (0,)))
        dq = dq + rows_of_heads(dq_far_ref, block_rows(row), lanes[c])
        store_heads(dq_rows, block_rows(row), lanes[c], (dq * INV_ROOT).astype(jnp.bfloat16))
        add_to(total_v, (row, g), dot(go[i], weights[i], ((0,), (0,))))
        add_to(total_k, (row, g), dot(rows_of_heads(q_ref, block_rows(row), lanes[c]), dscores[i], ((0,), (0,))))
        if (c + 1) * kv_heads // parts == g + 1:
            settle(row, g)
        if c == parts - 1:
            copy = pltpu.make_async_copy(
                dq_rows.at[block_rows(row), :], dq_ref.at[block_rows(row), :], sem.at[1 + row]
            )
            copy.start()
            copies.append(copy)

    def settle(row, g):
        for total, acc, part, scale in ((total_k, acc_k, 0, INV_ROOT), (total_v, acc_v, 1, None)):
            value = total[row, g]
            if row < per_shard - 1:
                value = value + acc[g, :, pl.ds(0, (row + 1) * BLOCK)]
            if row:
                acc[g, :, pl.ds(0, row * BLOCK)] = value[:, : row * BLOCK]
            done = value[:, row * BLOCK :]
            done = (done if scale is None else done * scale).astype(jnp.bfloat16).T
            own_ref[part, block_rows(row), heads_at[g]] = done

    skewed(len(chunks), [stage_dprobs, stage_dscores, stage_grads])
    for part, dst in enumerate((dk_ref, dv_ref)):
        copy = pltpu.make_async_copy(own_ref.at[part], dst, sem.at[1 + per_shard + part])
        copy.start()
        copies.append(copy)
    for copy in copies:
        copy.wait()


def known_top(shifted_ref, top_ref, rows, lanes):
    return jnp.where(shifted_ref[0] == 1, rows_of_heads(top_ref, rows, lanes), 0.0)


def finish(rows, lanes, go_ref, out, inv_norm, near, o_ref, go_near_ref, delta_ref):
    store_heads(o_ref, rows, lanes, out.astype(jnp.bfloat16))
    scaled = (rows_of_heads(go_ref, rows, lanes).astype(jnp.float32) * inv_norm).astype(jnp.bfloat16)
    exact = scaled.astype(jnp.float32)
    delta = jnp.sum(exact * out, axis=1, keepdims=True)
    if near is None:
        store_heads(go_near_ref, rows, lanes, scaled)
        store_heads(delta_ref, rows, lanes, jnp.broadcast_to(delta, out.shape))
    else:
        store_heads(go_near_ref, rows, lanes, (exact * near).astype(jnp.bfloat16))
        store_heads(delta_ref, rows, lanes, delta * near)
    return scaled, delta


def only_local(rows, lanes, go_ref, part_ref, norm_ref, o_ref, go_near_ref, delta_ref):
    for of in lanes:
        inv_norm = 1.0 / rows_of_heads(norm_ref, rows, of)
        out = rows_of_heads(part_ref, rows, of) * inv_norm
        finish(rows, of, go_ref, out, inv_norm, None, o_ref, go_near_ref, delta_ref)


def repeat(value, times):
    return jnp.concatenate([value] * times, axis=1)


def with_far(
    slots, kv_heads, rows, shifted_ref, q_ref, go_ref, part_ref, top_ref, norm_ref, far_ref, o_ref, dq_ref, go_near_ref, delta_ref,
    kt_t, vt_t, acc_k, acc_v, pos, lens,
):
    lanes = head_lanes(q_ref.shape[1])
    parts = len(lanes)
    kv = [c * kv_heads // parts for c in range(parts)]
    masks = far_masks(CHUNK, lens)
    k_cat = [table_rows(far_ref.at[0], g, pos) for g in range(kv_heads)]
    v_one = [with_ones(table_rows(far_ref.at[1], g, pos)) for g in range(kv_heads)]
    k_cat_t = [table_lanes(kt_t, g, pos) for g in range(kv_heads)]
    v_cat_t = [table_lanes(vt_t, g, pos) for g in range(kv_heads)]
    q, scores, top, near, weights, summed, scaled, delta, dprobs, dscores = ([None] * parts for _ in range(10))
    total_v, total_k = {}, {}

    def stage_scores(c):
        q[c] = rows_of_heads(q_ref, rows, lanes[c])
        scores[c] = dot(q[c], k_cat_t[kv[c]], ((1,), (0,)))

    def stage_weights(c):
        seen = hide(masks, scores[c])
        top_near = known_top(shifted_ref, top_ref, rows, lanes[c])
        top[c] = jnp.maximum(jnp.ceil(jnp.max(seen, axis=1, keepdims=True) * EXP2_SCALE), top_near)
        near[c] = jnp.exp2(top_near - top[c])
        weights[c] = jnp.exp2(seen * EXP2_SCALE - repeat(top[c], slots)).astype(jnp.bfloat16)

    def stage_summed(c):
        summed[c] = dot(weights[c], v_one[kv[c]], ((1,), (0,)))

    def stage_out(c):
        inv_norm = 1.0 / (near[c] * rows_of_heads(norm_ref, rows, lanes[c]) + summed[c][:, HEAD_SIZE:])
        out = (rows_of_heads(part_ref, rows, lanes[c]) * near[c] + summed[c][:, :HEAD_SIZE]) * inv_norm
        scaled[c], delta[c] = finish(rows, lanes[c], go_ref, out, inv_norm, near[c], o_ref, go_near_ref, delta_ref)

    def stage_dprobs(c):
        dprobs[c] = dot(scaled[c], v_cat_t[kv[c]], ((1,), (0,)))

    def stage_dscores(c):
        dscores[c] = (weights[c] * (dprobs[c] - delta[c]).astype(jnp.bfloat16))

    def stage_grads(c):
        store_heads(dq_ref, rows, lanes[c], dot(dscores[c], k_cat[kv[c]], ((1,), (0,))))
        add_to(total_v, kv[c], dot(scaled[c], weights[c], ((0,), (0,))))
        add_to(total_k, kv[c], dot(q[c], dscores[c], ((0,), (0,))))

    skewed(
        parts,
        [stage_scores, stage_weights, stage_summed, stage_out, stage_dprobs, stage_dscores, stage_grads],
    )
    for g in range(kv_heads):
        accumulate(acc_v, g, pos, total_v[g])
        accumulate(acc_k, g, pos, total_k[g])


def flip_table(src, dst, kv_heads, count):
    for g in range(kv_heads):
        for i in range(count):
            dst[g, i] = src[pl.ds(i * BLOCK, BLOCK), pl.ds(g * HEAD_SIZE, HEAD_SIZE)].T


def flush(acc, dst, kv_heads, count, scale):
    for g in range(kv_heads):
        for i in range(count):
            value = acc[g, i] if scale is None else acc[g, i] * scale
            dst[pl.ds(i * BLOCK, BLOCK), pl.ds(g * HEAD_SIZE, HEAD_SIZE)] = value.astype(jnp.bfloat16).T


def step_rows():
    row = pl.program_id(0)
    return row, pl.ds(pl.multiple_of(row * BLOCK, BLOCK), BLOCK)


def for_slots(plan_ref, at, most, vis, run):
    size = plan_ref[at]
    for slots in range(1, most + 1):

        @pl.when(size == slots)
        def _():
            pos = [plan_ref[at + 1 + slot] for slot in range(slots)]
            lens = [plan_ref[at + 1 + vis + slot] for slot in range(slots)]
            run(slots, pos, lens)


def far_kernel(
    ctx_size, per_shard, vis, plan_ref, shifted_ref, q_ref, go_ref, part_ref, top_ref, norm_ref, far_ref,
    o_ref, dq_ref, delta_ref, go_near_ref, dfar_ref, kt_t, vt_t, acc_k, acc_v,
):
    row, rows = step_rows()
    far = CAP * (ctx_size - 1)
    kv_heads = far_ref.shape[2] // HEAD_SIZE
    at = (per_shard + row) * plan_width(vis)

    @pl.when(row == 0)
    def _():
        flip_table(far_ref.at[0], kt_t, kv_heads, far)
        flip_table(far_ref.at[1], vt_t, kv_heads, far)
        acc_k[...] = jnp.zeros_like(acc_k)
        acc_v[...] = jnp.zeros_like(acc_v)

    @pl.when(plan_ref[at] == 0)
    def _():
        only_local(rows, head_lanes(go_ref.shape[1]), go_ref, part_ref, norm_ref, o_ref, go_near_ref, delta_ref)
        dq_ref[rows, :] = jnp.zeros((BLOCK, dq_ref.shape[1]), dq_ref.dtype)

    def run(slots, pos, lens):
        with_far(
            slots, kv_heads, rows, shifted_ref, q_ref, go_ref, part_ref, top_ref, norm_ref, far_ref, o_ref, dq_ref, go_near_ref, delta_ref,
            kt_t, vt_t, acc_k, acc_v, pos, lens,
        )

    for_slots(plan_ref, at, min(vis - 1, far), vis, run)

    @pl.when(row == pl.num_programs(0) - 1)
    def _():
        flush(acc_k, dfar_ref.at[0], kv_heads, far, INV_ROOT)
        flush(acc_v, dfar_ref.at[1], kv_heads, far, None)


def far_blocks(per_shard, vis, blocks_ref, count_ref, reader, owner):
    first, second = jnp.int32(per_shard), jnp.int32(-1)
    for row in range(per_shard):
        at = reader * per_shard + row
        count = count_ref[at]
        for slot in range(1, vis):
            of, index = split(blocks_ref[at, slot], per_shard)
            take = (slot < count) & (of == owner)
            first = jnp.minimum(first, jnp.where(take, index, per_shard))
            second = jnp.maximum(second, jnp.where(take, index, -1))
    return jnp.minimum(first, per_shard - 1), jnp.maximum(second, 0), second >= 0


def pack_pair_kernel(per_shard, vis, blocks_ref, count_ref, k_ref, v_ref, *rest):
    *out_refs, wide_ref, sem = rest
    me = lax.axis_index("ctx")

    @pl.when(me == 0)
    def _():
        first, second, _ = far_blocks(per_shard, vis, blocks_ref, count_ref, 1, 0)
        copies = []
        for place, index in enumerate((first, second)):
            rows = pl.ds(pl.multiple_of(index * BLOCK, BLOCK), BLOCK)
            for part, ref in enumerate((k_ref, v_ref)):
                copies.append(
                    pltpu.make_async_copy(
                        ref.at[rows, :], wide_ref.at[part, block_rows(place), :], sem.at[place, part]
                    )
                )
        for copy in copies:
            copy.start()
        for copy in copies:
            copy.wait()
        for g, out_ref in enumerate(out_refs):
            out_ref[:, 0] = wide_ref[:, :, pl.ds(g * HEAD_SIZE, HEAD_SIZE)]


def add_pair_kernel(
    per_shard, vis, blocks_ref, count_ref, own_ref, *rest
):
    *recv_refs, _, _, gk_ref, gv_ref, total_ref, sem = rest

    @pl.when(lax.axis_index("ctx") == 0)
    def _():
        first, second, _ = far_blocks(per_shard, vis, blocks_ref, count_ref, 1, 0)
        same = first == second
        copies = []
        for place, index in enumerate((first, second)):
            rows = pl.ds(pl.multiple_of(index * BLOCK, BLOCK), BLOCK)
            for part, dst in enumerate((gk_ref, gv_ref)):
                for g, recv_ref in enumerate(recv_refs):
                    lanes = pl.ds(g * HEAD_SIZE, HEAD_SIZE)
                    got = [recv_ref[part, 0, block_rows(p), :].astype(jnp.float32) for p in (place, 1 - place)]
                    total = own_ref[part, rows, lanes].astype(jnp.float32) + got[0] + jnp.where(same, got[1], 0.0)
                    total_ref[part, block_rows(place), lanes] = total.astype(jnp.bfloat16)
                copy = pltpu.make_async_copy(
                    total_ref.at[part, block_rows(place), :], dst.at[rows, :], sem.at[place, part]
                )
                copies.append((place, copy))

        def each(act):
            for place, copy in copies:
                if place == 0:
                    act(copy)
                else:
                    pl.when(jnp.logical_not(same))(functools.partial(act, copy))

        each(lambda copy: copy.start())
        each(lambda copy: copy.wait())


def far_pair_kernel(
    per_shard, vis, kv_heads, g, blocks_ref, count_ref, lens_ref, shifted_ref, q_ref, go_ref, part_ref, top_ref, norm_ref,
    far_ref, *rest
):
    o_ref, dq_ref, delta_ref, go_near_ref, dfar_ref, again_ref = rest[-6:]
    me = lax.axis_index("ctx")
    lanes = head_lanes(q_ref.shape[1])
    per_kv = len(lanes) // kv_heads
    lanes = lanes[g * per_kv : (g + 1) * per_kv]
    all_lanes = pl.ds(g * per_kv * CHUNK * HEAD_SIZE, per_kv * CHUNK * HEAD_SIZE)
    first, second, some = far_blocks(per_shard, vis, blocks_ref, count_ref, me, me - 1)

    @pl.when(jnp.logical_not(some))
    def _():
        for row in range(per_shard):
            only_local(block_rows(row), lanes, go_ref, part_ref, norm_ref, o_ref, go_near_ref, delta_ref)
        dq_ref[:, all_lanes] = jnp.zeros((dq_ref.shape[0], all_lanes.size), dq_ref.dtype)
        dfar_ref[...] = jnp.zeros_like(dfar_ref)

    again_ref[0] = jnp.where(some, shifted_ref[0], 0)
    earlier = (me - 1) * per_shard
    masks = []
    for row in range(per_shard):
        at = me * per_shard + row
        count = count_ref[at]
        lens = [jnp.int32(0), jnp.int32(0)]
        for slot in range(1, vis):
            block, visible = blocks_ref[at, slot], lens_ref[at, slot]
            live = slot < count
            lens[0] = lens[0] + jnp.where(live & (block == earlier + first), visible, 0)
            lens[1] = lens[1] + jnp.where(live & (block == earlier + second) & (first != second), visible, 0)
        masks.append(far_masks(CHUNK, lens))
    k, v = far_ref[0], far_ref[1]

    @pl.when(some & (shifted_ref[0] == 0))
    def _():
        k_t, v_t, v_one = k.T, v.T, with_ones(v)
        chunks = [(row, c) for row in range(per_shard) for c in range(per_kv)]
        q, scores, weights, summed, scaled, delta, dprobs, dscores = ([None] * len(chunks) for _ in range(8))
        total = {}
        bound = [None]

        def stage_scores(i):
            row, c = chunks[i]
            q[i] = rows_of_heads(q_ref, block_rows(row), lanes[c])
            scores[i] = dot(q[i], k_t, ((1,), (0,)))

        def stage_weights(i):
            weights[i] = jnp.exp2(hide(masks[chunks[i][0]], scores[i]) * EXP2_SCALE).astype(jnp.bfloat16)

        def stage_summed(i):
            summed[i] = dot(weights[i], v_one, ((1,), (0,)))

        def stage_out(i):
            row, c = chunks[i]
            rows = block_rows(row)
            norm = rows_of_heads(norm_ref, rows, lanes[c]) + summed[i][:, HEAD_SIZE:]
            bound[0] = norm if i == 0 else jnp.maximum(bound[0], norm)
            inv_norm = 1.0 / norm
            out = (rows_of_heads(part_ref, rows, lanes[c]) + summed[i][:, :HEAD_SIZE]) * inv_norm
            scaled[i], delta[i] = finish(rows, lanes[c], go_ref, out, inv_norm, None, o_ref, go_near_ref, delta_ref)

        def stage_dprobs(i):
            dprobs[i] = dot(scaled[i], v_t, ((1,), (0,)))

        def stage_dscores(i):
            dscores[i] = weights[i] * (dprobs[i] - delta[i]).astype(jnp.bfloat16)

        def stage_grads(i):
            row, c = chunks[i]
            store_heads(dq_ref, block_rows(row), lanes[c], dot(dscores[i], k, ((1,), (0,))))
            add_to(total, 1, dot(scaled[i], weights[i], ((0,), (0,))))
            add_to(total, 0, dot(q[i], dscores[i], ((0,), (0,))))

        skewed(
            len(chunks),
            [stage_scores, stage_weights, both(stage_summed, stage_out), both(stage_dprobs, stage_dscores), stage_grads],
        )
        dfar_ref[0] = (total[0] * INV_ROOT).astype(jnp.bfloat16).T
        dfar_ref[1] = total[1].astype(jnp.bfloat16).T
        again_ref[0] = jnp.where(jnp.max(bound[0]) < SUM_LIMIT, 0, 1).astype(jnp.int32)

    @pl.when(again_ref[0] == 1)
    def _():
        k_t, v_t, v_one = k.T, v.T, with_ones(v)
        total = (jnp.zeros((HEAD_SIZE, CAP * BLOCK), jnp.float32),) * 2
        for row in range(per_shard):
            rows = block_rows(row)

            def step(c, total):
                at = chunk_lanes(c)
                q = rows_of_heads(q_ref, rows, at)
                seen = hide(masks[row], dot(q, k_t, ((1,), (0,))))
                top_near = known_top(shifted_ref, top_ref, rows, at)
                top = jnp.maximum(jnp.ceil(jnp.max(seen, axis=1, keepdims=True) * EXP2_SCALE), top_near)
                near = jnp.exp2(top_near - top)
                weights = jnp.exp2(seen * EXP2_SCALE - repeat(top, CAP)).astype(jnp.bfloat16)
                summed = dot(weights, v_one, ((1,), (0,)))
                inv_norm = 1.0 / (near * rows_of_heads(norm_ref, rows, at) + summed[:, HEAD_SIZE:])
                out = (rows_of_heads(part_ref, rows, at) * near + summed[:, :HEAD_SIZE]) * inv_norm
                scaled, delta = finish(rows, at, go_ref, out, inv_norm, near, o_ref, go_near_ref, delta_ref)
                dprobs = dot(scaled, v_t, ((1,), (0,)))
                dscores = weights * (dprobs - delta).astype(jnp.bfloat16)
                store_heads(dq_ref, rows, at, dot(dscores, k, ((1,), (0,))))
                grads = dot(q, dscores, ((0,), (0,))), dot(scaled, weights, ((0,), (0,)))
                return total[0] + grads[0], total[1] + grads[1]

            total = lax.fori_loop(g * per_kv, (g + 1) * per_kv, step, total)
        dfar_ref[0] = (total[0] * INV_ROOT).astype(jnp.bfloat16).T
        dfar_ref[1] = total[1].astype(jnp.bfloat16).T


def body(ctx_size, query_states, key_states, value_state_rows, grad_out, vis_blocks, vis_count, vis_len):
    tokens, q_width = query_states.shape
    kv_width = key_states.shape[1]
    heads = kv_width // HEAD_SIZE
    per_shard = tokens // BLOCK
    vis = vis_blocks.shape[1]
    far = CAP * (ctx_size - 1)
    smem = pl.BlockSpec(memory_space=pltpu.SMEM)
    vmem = pl.BlockSpec(memory_space=pltpu.VMEM)
    hbm = pl.BlockSpec(memory_space=pltpu.HBM)
    bf16 = jnp.bfloat16
    pin = lambda array: pltpu.with_memory_space_constraint(array, pltpu.HBM)
    pair = ctx_size == 2
    sent_type = jax.ShapeDtypeStruct((2, ctx_size - 1, CAP * BLOCK, kv_width), bf16)
    busy = pl.CostEstimate(flops=10**10, bytes_accessed=2**20, transcendentals=0)
    small = pltpu.CompilerParams(vmem_limit_bytes=SMALL_VMEM)
    if pair:
        sent = pl.pallas_call(
            functools.partial(pack_pair_kernel, per_shard, vis),
            out_shape=[jax.ShapeDtypeStruct((2, 1, CAP * BLOCK, HEAD_SIZE), bf16)] * heads,
            in_specs=[smem, smem, hbm, hbm],
            out_specs=[vmem] * heads,
            scratch_shapes=[pltpu.VMEM((2, CAP * BLOCK, kv_width), bf16), pltpu.SemaphoreType.DMA((CAP, 2))],
            compiler_params=small,
            cost_estimate=busy,
            name="pack",
        )(pin(vis_blocks), pin(vis_count), pin(key_states), pin(value_state_rows))
    else:
        sent, plan = pl.pallas_call(
            functools.partial(pack_kernel, ctx_size, per_shard, vis),
            out_shape=[sent_type, jax.ShapeDtypeStruct((plan_size(ctx_size, per_shard, vis),), jnp.int32)],
            in_specs=[smem, smem, smem, hbm, hbm],
            out_specs=[vmem, smem],
            scratch_shapes=[
                pltpu.SMEM((ctx_size,), jnp.int32),
                pltpu.SemaphoreType.DMA((ctx_size - 1, per_shard, 2)),
            ],
            compiler_params=small,
            cost_estimate=busy,
            name="pack",
        )(pin(vis_blocks), pin(vis_count), pin(vis_len), pin(key_states), pin(value_state_rows))

    def move(array, back):
        parts = []
        for shift in range(1, ctx_size):
            pairs = [(i, i + shift) for i in range(ctx_size - shift)]
            if back:
                pairs = [(b, a) for a, b in pairs]
            parts.append(lax.ppermute(array[:, shift - 1 : shift], "ctx", pairs))
        return parts[0] if len(parts) == 1 else jnp.concatenate(parts, axis=1)

    if pair:
        got = [move(array, False).reshape(2, far * BLOCK, HEAD_SIZE) for array in reversed(sent)][::-1]
    else:
        got = move(sent, False).reshape(2, far * BLOCK, kv_width)
    q_type = jax.ShapeDtypeStruct(query_states.shape, bf16)
    part_type = jax.ShapeDtypeStruct(query_states.shape, jnp.float32)
    kv_type = jax.ShapeDtypeStruct(key_states.shape, bf16)
    weights_type = jax.ShapeDtypeStruct((q_width, per_shard * (per_shard + 1) // 2 * BLOCK), bf16)
    flipped = lambda n, kind: pltpu.VMEM((heads, n, HEAD_SIZE, BLOCK), kind)
    large = pltpu.CompilerParams(vmem_limit_bytes=LARGE_VMEM + far // 4 * 2**20)
    flops = 2 * tokens * tokens * q_width
    cost = lambda n: pl.CostEstimate(flops=n * flops, bytes_accessed=8 * 2**20, transcendentals=0)
    lists = (pin(vis_blocks), pin(vis_count), pin(vis_len))
    part, top, norm, weights, shifted = pl.pallas_call(
        functools.partial(forward_kernel, ctx_size, per_shard, vis),
        out_shape=[part_type] * 3 + [weights_type, jax.ShapeDtypeStruct((1,), jnp.int32)],
        in_specs=[smem] * 3 + [vmem] * 3,
        out_specs=[vmem] * 4 + [smem],
        compiler_params=large,
        cost_estimate=pl.CostEstimate(flops=2**20, bytes_accessed=2**20, transcendentals=0),
        name="forward_local",
    )(*lists, query_states, key_states, value_state_rows)
    far_types = [q_type, part_type, part_type, q_type]
    if pair:
        dfar, before = [], []
        for g in range(heads):
            *before, array = pl.pallas_call(
                functools.partial(far_pair_kernel, per_shard, vis, heads, g),
                out_shape=far_types + [jax.ShapeDtypeStruct(got[g].shape, bf16)],
                in_specs=[smem] * 4 + [vmem] * (6 + len(before)),
                out_specs=[vmem] * 5,
                scratch_shapes=[pltpu.SMEM((1,), jnp.int32)],
                input_output_aliases={10 + i: i for i in range(len(before))},
                compiler_params=large,
                cost_estimate=cost(3),
                name="far",
            )(*lists, shifted, query_states, grad_out, part, top, norm, got[g], *before)
            dfar.append(array)
        attention, dq_far, delta, go_near = before
    else:
        attention, dq_far, delta, go_near, dfar = pl.pallas_call(
            functools.partial(far_kernel, ctx_size, per_shard, vis),
            out_shape=far_types + [jax.ShapeDtypeStruct(got.shape, bf16)],
            grid_spec=pltpu.PrefetchScalarGridSpec(
                num_scalar_prefetch=2,
                grid=(per_shard,),
                in_specs=[vmem] * 6,
                out_specs=[vmem] * 5,
                scratch_shapes=[flipped(far, bf16)] * 2 + [flipped(far, jnp.float32)] * 2,
            ),
            compiler_params=large,
            cost_estimate=cost(6),
            name="far",
        )(plan, shifted, query_states, grad_out, part, top, norm, got)
    if pair:
        returned = [move(array.reshape(2, 1, CAP * BLOCK, HEAD_SIZE), True) for array in dfar]
    else:
        returned = [move(dfar.reshape(sent.shape), True)]
    earlier = returned[:-1]
    own, attention, grad_query, dk, dv = pl.pallas_call(
        functools.partial(backward_kernel, ctx_size, per_shard, vis),
        out_shape=[jax.ShapeDtypeStruct((2, tokens, kv_width), bf16), q_type, q_type, kv_type, kv_type],
        in_specs=[vmem] * (8 + len(earlier)),
        out_specs=[vmem] + [hbm] * 4,
        scratch_shapes=[pltpu.VMEM((heads, HEAD_SIZE, tokens), jnp.float32)] * 2
        + [pltpu.VMEM(query_states.shape, bf16), pltpu.SemaphoreType.DMA((3 + per_shard,))],
        compiler_params=large,
        cost_estimate=cost(5),
        name="backward_local",
    )(query_states, go_near, dq_far, delta, weights, key_states, value_state_rows, attention, *earlier)
    add, lists = (add_pair_kernel, lists[:2]) if pair else (functools.partial(add_kernel, ctx_size), (plan,))
    grad_key, grad_value = pl.pallas_call(
        functools.partial(add, per_shard, vis),
        out_shape=[kv_type, kv_type],
        in_specs=[smem] * len(lists) + [vmem] * (1 + len(returned)) + [hbm, hbm],
        out_specs=[hbm, hbm],
        scratch_shapes=[
            pltpu.VMEM((2, tokens, kv_width), bf16),
            pltpu.SemaphoreType.DMA((2, per_shard)),
        ],
        input_output_aliases={len(lists) + len(returned) + 1: 0, len(lists) + len(returned) + 2: 1},
        compiler_params=small,
        name="add",
    )(*lists, own, *returned, dk, dv)
    return attention, grad_query, grad_key, grad_value


def solution(mesh):
    rows = P(("dp", "ctx"), "head")
    return jax.shard_map(
        functools.partial(body, mesh.shape["ctx"]),
        mesh=mesh,
        in_specs=(rows, rows, rows, rows, P("dp", None), P("dp"), P("dp", None)),
        out_specs=(rows, rows, rows, rows),
        check_vma=False,
    )
```
